512 devices in a mesh: ctx: 64 (over y, z_lo, x), isl: 8 (over z_hi, core).
Axes of the slice: x: 4, y: 4, z: 16 (z_hi: 4, z_lo: 4; z = z_hi * 4 + z_lo), core: 2. Of those that a mesh axis runs over, the one named last changes fastest.
Arguments:
- layer_input: bfloat16 [8, 16384, 4096], P('isl', 'ctx'), may hold values from -6 to 6
- queries: bfloat16 [8, 16384, 1024], P('isl', 'ctx'), may hold values from -110 to 110
- grad_out: bfloat16 [8, 16384, 1024], P('isl', 'ctx'), may hold values from -6 to 6
- key_weight: bfloat16 [4096, 128], P(('ctx', 'isl')), may hold values from -0.09375 to 0.09375
- value_weight: bfloat16 [4096, 128], P(('ctx', 'isl')), may hold values from -0.09375 to 0.09375
- doc_len: int32 [8, 85], P('isl'), may hold values from 1 to 8, 256 in all within a row
Outputs:
- attn_out: bfloat16 [8, 16384, 1024], P('isl', 'ctx')
- grad_queries: bfloat16 [8, 16384, 1024], P('isl', 'ctx')
- grad_key_weight: float32 [4096, 128], P(('ctx', 'isl'))
- grad_value_weight: float32 [4096, 128], P(('ctx', 'isl'))
The draws below stay inside these ranges and needn't reach their ends.
Inputs may be any that keep to these rules, and one draw needn't show every extreme that they name: `doc_len`: lengths in units of 64 tokens; those of one sequence sum to 256, and the longest of each sequence is exactly 8.
All inputs are finite; a program needn't handle non-finite values.
Results may differ from the reference program's by a relative error of at most 0.034.
The reference program's roundings to bfloat16 on the way (of `keys`, `probs_low`, `dscores`, `grad_keys` and `grad_values`) count: a program that leaves them out, or rounds other values in their place, can miss the bound.
Values may be sent and summed in bfloat16 or wider, within the bound.
No kernel may reach another device: no remote copies, remote signals or barrier semaphores. Data moves between devices by JAX's collectives and lax.ppermute only.
A program may use at most 64 MiB of HBM per device.

```python
import math
import jax
import jax.numpy as jnp
import numpy as np
from jax import lax

D = 4096
HD = 128
QPK = 8
GROUPS = 1
ROWS = 256
QW = 1024
KW = 128
SEQS = 8
SEQ = 16384
SLOT = 8
NDOC = 85
N_CTX = 64
N_ISL = 8


def draw_queries(key, part):
    key = jax.random.fold_in(key, 11)
    first = jax.random.fold_in(key, 0)
    return jnp.clip(jax.random.normal(first, (SEQS, SEQ, QW), jnp.float32), -6.0, 6.0).astype(jnp.bfloat16)


def steps_of(own_key, extent, cuts, least, high):
    loudness = 1.0
    for position, shards_of in cuts:
        steps = jax.random.uniform(jax.random.fold_in(jax.random.fold_in(own_key, 6), position), (shards_of,), jnp.float32, least / len(cuts), high / len(cuts))
        loudness = loudness * jnp.repeat(jnp.exp(steps), extent[position] // shards_of).reshape((-1,) + (1,) * (len(extent) - 1 - position))
    return loudness


def split_up(count, total, limit, skew):
    loads = [(1 << 20) // math.isqrt(grade ** skew) + 1 for grade in range(2, count + 1)]
    rest, holding = total - limit - (count - 1), [1] * (count - 1)
    while rest > 0:
        candidates = [i for i in range(count - 1) if holding[i] < limit]
        pool, left = sum([loads[i] for i in candidates]), rest
        for i in candidates:
            extra = min(limit - holding[i], max(1, left * loads[i] // pool), rest)
            holding[i] = holding[i] + extra
            rest = rest - extra
    return np.array([limit] + holding)


def uneven_parts(key, count, total, bound, lean):
    if count == 2:
        one = jax.random.randint(key, (), max(1, total - bound), min(bound, total - 1) + 1)
        return jnp.stack([one, total - one])
    sizes = jnp.asarray(split_up(count, total, bound, lean), jnp.int32)
    pairs = (count - 1) // 2
    giver, taker = sizes[1:1 + 2 * pairs:2], sizes[2:2 + 2 * pairs:2]
    room = jnp.minimum(giver - 1, bound - taker)
    passed = jax.random.randint(jax.random.fold_in(key, 1), (pairs,), 0, 1 << 20) % (room + 1)
    sizes = sizes.at[1:1 + 2 * pairs:2].set(giver - passed).at[2:2 + 2 * pairs:2].set(taker + passed)
    return sizes[jax.random.permutation(jax.random.fold_in(key, 2), count)]


def scatter_about(rng, shape, deviation, most, shards=(), kind=jnp.bfloat16):
    entries = deviation * jax.random.normal(rng, shape, jnp.float32)
    if shards:
        entries = entries * steps_of(rng, shape, shards, -0.22, 0.18)
    return jnp.clip(entries, -most, most).astype(kind)


def setup_inputs(seed: int = 0) -> dict:
    seeds = jax.random.split(jax.random.key(seed), 7)
    return {
        "layer_input": scatter_about(seeds[0], (SEQS, SEQ, D), 1.0, 6.0, ((0, 8), (1, 64))),
        "queries": draw_queries(jax.random.fold_in(seeds[6], 71), 0),
        "grad_out": scatter_about(seeds[2], (SEQS, SEQ, QW), 1.0, 6.0, ((0, 8), (1, 64))),
        "key_weight": scatter_about(seeds[3], (D, KW), D ** -0.5, 0.09375, ((0, 512),)),
        "value_weight": scatter_about(seeds[4], (D, KW), D ** -0.5, 0.09375, ((0, 512),)),
        "doc_len": jax.vmap(lambda own: uneven_parts(own, NDOC, ROWS, SLOT, 2))(jax.random.split(seeds[5], SEQS)).reshape((SEQS, NDOC)).astype(jnp.int32),
    }


def stored(value):
    return lax.optimization_barrier(value.astype(jnp.bfloat16)).astype(jnp.float32)


def unit_documents(lengths):
    ends = jnp.cumsum(lengths).astype(jnp.int32)
    begins = ends - lengths
    units = jnp.arange(ROWS, dtype=jnp.int32)
    numbers = jnp.arange(lengths.shape[0], dtype=jnp.int32)
    inside = (units[:, None] >= begins[None, :]) & (units[:, None] < ends[None, :])
    return jnp.sum(jnp.where(inside, numbers[None, :], 0), axis=1).astype(jnp.int32)


def by_unit(array):
    return array.reshape(N_CTX, ROWS, array.shape[-1]).transpose(1, 0, 2)


def by_storage(array):
    return array.transpose(1, 0, 2).reshape(N_CTX * ROWS, array.shape[-1])


def one_sequence(inputs, query_rows, grad_rows, key_weight, value_weight, lengths):
    scale = float(HD) ** -0.5
    key_rows = jnp.dot(inputs, key_weight, preferred_element_type=jnp.float32).astype(jnp.bfloat16)
    value_rows = jnp.dot(inputs, value_weight, preferred_element_type=jnp.float32).astype(jnp.bfloat16)
    queries_unit = by_unit(query_rows).reshape(ROWS, N_CTX, GROUPS, QPK, HD)
    grads_unit = by_unit(grad_rows).reshape(ROWS, N_CTX, GROUPS, QPK, HD)
    margin = SLOT - 1
    keys_pad = jnp.concatenate([jnp.zeros((margin, N_CTX, GROUPS * HD), jnp.bfloat16), by_unit(key_rows)], axis=0)
    values_pad = jnp.concatenate([jnp.zeros((margin, N_CTX, GROUPS * HD), jnp.bfloat16), by_unit(value_rows)], axis=0)
    documents = unit_documents(lengths)
    documents_pad = jnp.concatenate([jnp.full((margin,), -1, jnp.int32), documents])
    window = SLOT * N_CTX
    offsets = jnp.arange(window, dtype=jnp.int32)
    columns = jnp.arange(N_CTX, dtype=jnp.int32)

    def visit(carry, unit):
        key_acc, value_acc = carry
        query = queries_unit[unit].astype(jnp.float32)
        grad = grads_unit[unit].astype(jnp.float32)
        keys = lax.dynamic_slice_in_dim(keys_pad, unit, SLOT, 0).reshape(window, GROUPS, HD).astype(jnp.float32)
        values = lax.dynamic_slice_in_dim(values_pad, unit, SLOT, 0).reshape(window, GROUPS, HD).astype(jnp.float32)
        key_doc = jnp.repeat(lax.dynamic_slice_in_dim(documents_pad, unit, SLOT, 0), N_CTX)
        key_pos = (unit - margin) * N_CTX + offsets
        query_pos = unit * N_CTX + columns
        allowed = (key_doc[None, :] == documents[unit]) & (key_pos[None, :] <= query_pos[:, None])
        scores = jnp.einsum('qgph,kgh->gpqk', query, keys) * scale
        scores = jnp.where(allowed[None, None], scores, -jnp.inf)
        peak = jnp.max(scores, axis=-1, keepdims=True)
        expo = jnp.exp(scores - peak)
        probs = expo / jnp.sum(expo, axis=-1, keepdims=True)
        probs_low = stored(probs)
        output = jnp.einsum('gpqk,kgh->qgph', probs_low, values).astype(jnp.bfloat16)
        delta = jnp.sum(grad * output.astype(jnp.float32), axis=-1)
        dprobs = jnp.einsum('qgph,kgh->gpqk', grad, values)
        dscores = stored(probs * (dprobs - jnp.transpose(delta, (1, 2, 0))[..., None]))
        dquery = (jnp.einsum('gpqk,kgh->qgph', dscores, keys) * scale).astype(jnp.bfloat16)
        dkeys = jnp.einsum('gpqk,qgph->kgh', dscores, query) * scale
        dvalues = jnp.einsum('gpqk,qgph->kgh', probs_low, grad)
        old_keys = lax.dynamic_slice_in_dim(key_acc, unit, SLOT, 0)
        old_values = lax.dynamic_slice_in_dim(value_acc, unit, SLOT, 0)
        key_acc = lax.dynamic_update_slice_in_dim(key_acc, old_keys + dkeys.reshape(SLOT, N_CTX, GROUPS * HD), unit, 0)
        value_acc = lax.dynamic_update_slice_in_dim(value_acc, old_values + dvalues.reshape(SLOT, N_CTX, GROUPS * HD), unit, 0)
        return (key_acc, value_acc), (output, dquery)

    start = jnp.zeros((ROWS + margin, N_CTX, GROUPS * HD), jnp.float32)
    (key_acc, value_acc), (outputs, dqueries) = lax.scan(visit, (start, start), jnp.arange(ROWS, dtype=jnp.int32))
    attn = by_storage(outputs.reshape(ROWS, N_CTX, GROUPS * QPK * HD))
    dquery_rows = by_storage(dqueries.reshape(ROWS, N_CTX, GROUPS * QPK * HD))
    grad_keys = by_storage(key_acc[margin:].astype(jnp.bfloat16))
    grad_values = by_storage(value_acc[margin:].astype(jnp.bfloat16))
    key_grad = jnp.dot(inputs.T, grad_keys, preferred_element_type=jnp.float32)
    value_grad = jnp.dot(inputs.T, grad_values, preferred_element_type=jnp.float32)
    return attn, dquery_rows, key_grad, value_grad


def reference(layer_input, queries, grad_out, key_weight, value_weight, doc_len):
    attn_all = []
    dquery_all = []
    key_total = jnp.zeros((D, GROUPS * HD), jnp.float32)
    value_total = jnp.zeros((D, GROUPS * HD), jnp.float32)
    for sequence in range(N_ISL):
        attn, dquery_rows, key_grad, value_grad = one_sequence(layer_input[sequence], queries[sequence], grad_out[sequence], key_weight, value_weight, doc_len[sequence])
        attn_all.append(attn)
        dquery_all.append(dquery_rows)
        key_total = key_total + key_grad
        value_total = value_total + value_grad
    return jnp.stack(attn_all), jnp.stack(dquery_all), key_total, value_total
```

```python
import math

import jax
import jax.numpy as jnp
from jax import lax
from jax.experimental import pallas as pl
from jax.experimental.pallas import tpu as pltpu
from jax.sharding import Mesh, PartitionSpec as P

HD = 128
QPK = 8
WIDTH = QPK * HD
COLS = 64
OWN = 4
BLOCKS = 3

SPLIT = ("y", "zl", "x", "zh", "core")
CTX = ("y", "zl", "x")
PLANE = ("y", "x")
LINE = ("zl", "zh")
last_dims = (((1,), (1,)), ((), ()))
plain_dims = (((1,), (0,)), ((), ()))
first_dims = (((0,), (0,)), ((), ()))
hidden = -1e30


def attention_kernel(begin_ref, first_ref, got_ref, back_ref, bias_ref, p_ref, ds_ref):
    rows = got_ref.shape[0]
    keys = BLOCKS * rows
    first = first_ref[0]
    scale = float(HD) ** -0.5
    factor = scale * math.log2(math.e)

    key_row = lax.broadcasted_iota(jnp.int32, (keys, 1), 0)
    key_block = key_row // rows
    key_col = (key_row - key_block * rows) // OWN
    key_unit = first + (key_block - (BLOCKS - 1)) * OWN + key_row % OWN
    key_pos = key_unit * COLS + key_col
    row = lax.broadcasted_iota(jnp.int32, (1, rows), 1)
    slot = row % OWN
    row_pos = (first + slot) * COLS + row // OWN
    start = jnp.zeros((1, rows), jnp.int32)
    for i in range(OWN):
        start = jnp.where(slot == i, begin_ref[i], start)
    allowed = (key_unit >= start) & (key_pos <= row_pos)
    bias_ref[...] = jnp.where(allowed, 0.0, hidden).astype(jnp.float32)

    def window(place):
        parts = [got_ref[:, 2 * WIDTH + (2 * k + place) * HD:][:, :HD] for k in range(BLOCKS)]
        return jnp.concatenate(parts, axis=0)

    key, value = window(0), window(1)
    key_t, value_t = key.T, value.T
    for head in range(QPK):
        cols = slice(head * HD, (head + 1) * HD)
        gcols = slice(WIDTH + head * HD, WIDTH + (head + 1) * HD)
        part = slice(head * rows, (head + 1) * rows)
        query = got_ref[:, cols]
        grad = got_ref[:, gcols]
        grad_t = grad.T.astype(jnp.float32)
        score = lax.dot_general(key, query, last_dims, preferred_element_type=jnp.float32)
        score = score * factor + bias_ref[...]
        expo = jnp.exp2(score - jnp.max(score, axis=0, keepdims=True))
        probs = expo * (1.0 / jnp.sum(expo, axis=0, keepdims=True))
        low = probs.astype(jnp.bfloat16)
        p_ref[:, part] = low
        out_t = lax.dot_general(value_t, low, plain_dims, preferred_element_type=jnp.float32)
        out_t = out_t.astype(jnp.bfloat16)
        back_ref[:, cols] = out_t.T
        delta = jnp.sum(grad_t * out_t.astype(jnp.float32), axis=0, keepdims=True)
        dprobs = lax.dot_general(value, grad, last_dims, preferred_element_type=jnp.float32)
        dscore = (probs * (dprobs - delta)).astype(jnp.bfloat16)
        ds_ref[:, part] = dscore
        dq_t = lax.dot_general(key_t, dscore, plain_dims, preferred_element_type=jnp.float32) * scale
        back_ref[:, gcols] = dq_t.astype(jnp.bfloat16).T
    for k in range(BLOCKS):
        block = slice(k * rows, (k + 1) * rows)
        dkey = jnp.zeros((rows, HD), jnp.float32)
        dvalue = jnp.zeros((rows, HD), jnp.float32)
        for head in range(QPK):
            cols = slice(head * HD, (head + 1) * HD)
            gcols = slice(WIDTH + head * HD, WIDTH + (head + 1) * HD)
            part = slice(head * rows, (head + 1) * rows)
            dkey += lax.dot_general(ds_ref[block, part], got_ref[:, cols], plain_dims, preferred_element_type=jnp.float32)
            dvalue += lax.dot_general(p_ref[block, part], got_ref[:, gcols], plain_dims, preferred_element_type=jnp.float32)
        at = 2 * WIDTH + 2 * k * HD
        back_ref[:, at:at + HD] = (dkey * scale).astype(jnp.bfloat16)
        back_ref[:, at + HD:at + 2 * HD] = dvalue.astype(jnp.bfloat16)


def attention(begins, first, got):
    rows = got.shape[0]
    keys = BLOCKS * rows
    vmem = pl.BlockSpec(memory_space=pltpu.VMEM)
    smem = pl.BlockSpec(memory_space=pltpu.SMEM)
    return pl.pallas_call(
        attention_kernel,
        out_shape=jax.ShapeDtypeStruct(got.shape, jnp.bfloat16),
        in_specs=[smem, smem, vmem],
        out_specs=vmem,
        scratch_shapes=[
            pltpu.VMEM((keys, rows), jnp.float32),
            pltpu.VMEM((keys, QPK * rows), jnp.bfloat16),
            pltpu.VMEM((keys, QPK * rows), jnp.bfloat16),
        ],
        compiler_params=pltpu.CompilerParams(vmem_limit_bytes=40 * 1024 * 1024),
        cost_estimate=pl.CostEstimate(
            flops=10 * rows * keys * HD * QPK, bytes_accessed=4 * got.size, transcendentals=rows * keys * QPK
        ),
    )(begins, first, got)


def exchange(array, axes):
    return lax.all_to_all(array, axes, split_axis=0, concat_axis=0, tiled=True)


def spread(array, axes):
    count = lax.axis_size(axes)
    return exchange(jnp.broadcast_to(array[None], (count,) + array.shape), axes)


def swap(array):
    return lax.ppermute(array, "core", [(0, 1), (1, 0)])


def later(array, steps):
    fill = jnp.zeros((steps, array.shape[1]), array.dtype)
    return jnp.concatenate([fill, array[:-steps]], axis=0)


def earlier(array, steps):
    fill = jnp.zeros((steps, array.shape[1]), array.dtype)
    return jnp.concatenate([array[steps:], fill], axis=0)


def gather_weights(weight):
    line = spread(weight, LINE)
    plane = spread(line, PLANE)
    other = swap(plane)
    core = lax.axis_index("core")
    both = jnp.where(core == 0, jnp.stack([plane, other]), jnp.stack([other, plane]))
    rows, width = weight.shape
    natural = both.reshape(2, 4, 4, 4, 4, rows, width).transpose(1, 3, 2, 4, 0, 5, 6)
    return natural.reshape(-1, width)


def reduce_weights(part):
    width = part.shape[1]
    rows = part.shape[0] // 512
    split = part.reshape(4, 4, 4, 4, 2, rows, width).transpose(4, 0, 2, 1, 3, 5, 6)
    core = jnp.sum(exchange(split.reshape(2, -1, width), "core"), axis=0)
    plane = jnp.sum(exchange(core.reshape(16, -1, width), PLANE), axis=0)
    return jnp.sum(exchange(plane.reshape(16, rows, width), LINE), axis=0)


def per_device(layer_input, queries, grad_out, key_weight, value_weight, doc_len):
    inputs = layer_input[0]
    place = lax.axis_index(CTX)
    ends = jnp.cumsum(doc_len[0])
    units = place * OWN + jnp.arange(OWN, dtype=jnp.int32)
    begins = jnp.max(jnp.where(ends[None, :] <= units[:, None], ends[None, :], 0), axis=1)
    first = (place * OWN).astype(jnp.int32).reshape(1)

    weight = gather_weights(jnp.concatenate([key_weight, value_weight], axis=1))
    kv = jnp.dot(inputs, weight, preferred_element_type=jnp.float32).astype(jnp.bfloat16)
    window = [kv if k == 0 else later(kv, k * OWN) for k in reversed(range(BLOCKS))]
    sent = jnp.concatenate([queries[0], grad_out[0]] + window, axis=1)
    got = exchange(sent, CTX)

    back = exchange(attention(begins, first, got), CTX)

    parts = [back[:, 2 * WIDTH + 2 * k * HD:][:, :2 * HD].astype(jnp.float32) for k in range(BLOCKS)]
    dkv = parts[BLOCKS - 1]
    for k in range(1, BLOCKS):
        dkv = dkv + earlier(parts[BLOCKS - 1 - k], k * OWN)
    grad = lax.dot_general(inputs, dkv.astype(jnp.bfloat16), first_dims, preferred_element_type=jnp.float32)
    share = reduce_weights(grad)
    return (back[None, :, :WIDTH], back[None, :, WIDTH:2 * WIDTH], share[:, :HD], share[:, HD:])


def solution(mesh):
    split = Mesh(mesh.devices.reshape(4, 4, 4, 4, 2), SPLIT)
    isl = ("zh", "core")
    placed = (
        P(isl, CTX, None),
        P(isl, CTX, None),
        P(isl, CTX, None),
        P(SPLIT, None),
        P(SPLIT, None),
        P(isl, None),
    )
    return jax.shard_map(
        per_device,
        mesh=split,
        in_specs=placed,
        out_specs=(
            P(isl, CTX, None),
            P(isl, CTX, None),
            P(SPLIT, None),
            P(SPLIT, None),
        ),
        check_vma=False,
    )
```

```python
import math

import jax
import jax.numpy as jnp
from jax import lax
from jax.experimental import pallas as pl
from jax.experimental.pallas import tpu as pltpu
from jax.sharding import Mesh, PartitionSpec as P

HD = 128
QPK = 8
WIDTH = QPK * HD
COLS = 64
OWN = 4
BLOCKS = 3

SPLIT = ("y", "zl", "x", "zh", "core")
CTX = ("y", "zl", "x")
PLANE = ("y", "x")
LINE = ("zl", "zh")
last_dims = (((1,), (1,)), ((), ()))
plain_dims = (((1,), (0,)), ((), ()))
first_dims = (((0,), (0,)), ((), ()))
hidden = -1e30
FEATURES = 2 * WIDTH + 2 * BLOCKS * HD
vmem = pl.BlockSpec(memory_space=pltpu.VMEM)
smem = pl.BlockSpec(memory_space=pltpu.SMEM)
roomy = pltpu.CompilerParams(vmem_limit_bytes=40 * 1024 * 1024)


def attention_kernel(begin_ref, first_ref, sent_ref, back_ref, got_ref, bias_ref, p_ref, ds_ref):
    rows = COLS * OWN
    keys = BLOCKS * rows
    first = first_ref[0]
    got_ref[...] = sent_ref[...].reshape(rows, FEATURES)
    scale = float(HD) ** -0.5
    factor = scale * math.log2(math.e)

    key_row = lax.broadcasted_iota(jnp.int32, (keys, 1), 0)
    key_block = key_row // rows
    key_col = (key_row - key_block * rows) // OWN
    key_unit = first + (key_block - (BLOCKS - 1)) * OWN + key_row % OWN
    key_pos = key_unit * COLS + key_col
    row = lax.broadcasted_iota(jnp.int32, (1, rows), 1)
    slot = row % OWN
    row_pos = (first + slot) * COLS + row // OWN
    start = jnp.zeros((1, rows), jnp.int32)
    for i in range(OWN):
        start = jnp.where(slot == i, begin_ref[i], start)
    allowed = (key_unit >= start) & (key_pos <= row_pos)
    bias_ref[...] = jnp.where(allowed, 0.0, hidden).astype(jnp.float32)

    def window(place):
        parts = [got_ref[:, 2 * WIDTH + (2 * k + place) * HD:][:, :HD] for k in range(BLOCKS)]
        return jnp.concatenate(parts, axis=0)

    key, value = window(0), window(1)
    key_t, value_t = key.T, value.T
    for head in range(QPK):
        cols = slice(head * HD, (head + 1) * HD)
        gcols = slice(WIDTH + head * HD, WIDTH + (head + 1) * HD)
        part = slice(head * rows, (head + 1) * rows)
        query = got_ref[:, cols]
        grad = got_ref[:, gcols]
        grad_t = grad.T.astype(jnp.float32)
        score = lax.dot_general(key, query, last_dims, preferred_element_type=jnp.float32)
        score = score * factor + bias_ref[...]
        expo = jnp.exp2(score - jnp.max(score, axis=0, keepdims=True))
        probs = expo * (1.0 / jnp.sum(expo, axis=0, keepdims=True))
        low = probs.astype(jnp.bfloat16)
        p_ref[:, part] = low
        out_t = lax.dot_general(value_t, low, plain_dims, preferred_element_type=jnp.float32)
        out_t = out_t.astype(jnp.bfloat16)
        back_ref[:, :, cols] = out_t.T.reshape(COLS, OWN, HD)
        delta = jnp.sum(grad_t * out_t.astype(jnp.float32), axis=0, keepdims=True)
        dprobs = lax.dot_general(value, grad, last_dims, preferred_element_type=jnp.float32)
        dscore = (probs * (dprobs - delta)).astype(jnp.bfloat16)
        ds_ref[:, part] = dscore
        dq_t = lax.dot_general(key_t, dscore, plain_dims, preferred_element_type=jnp.float32) * scale
        back_ref[:, :, gcols] = dq_t.astype(jnp.bfloat16).T.reshape(COLS, OWN, HD)
    for k in range(BLOCKS):
        block = slice(k * rows, (k + 1) * rows)
        dkey = jnp.zeros((rows, HD), jnp.float32)
        dvalue = jnp.zeros((rows, HD), jnp.float32)
        for head in range(QPK):
            cols = slice(head * HD, (head + 1) * HD)
            gcols = slice(WIDTH + head * HD, WIDTH + (head + 1) * HD)
            part = slice(head * rows, (head + 1) * rows)
            dkey += lax.dot_general(ds_ref[block, part], got_ref[:, cols], plain_dims, preferred_element_type=jnp.float32)
            dvalue += lax.dot_general(p_ref[block, part], got_ref[:, gcols], plain_dims, preferred_element_type=jnp.float32)
        at = 2 * WIDTH + 2 * k * HD
        back_ref[:, :, at:at + HD] = (dkey * scale).astype(jnp.bfloat16).reshape(COLS, OWN, HD)
        back_ref[:, :, at + HD:at + 2 * HD] = dvalue.astype(jnp.bfloat16).reshape(COLS, OWN, HD)


def attention(begins, first, sent):
    rows = COLS * OWN
    keys = BLOCKS * rows
    return pl.pallas_call(
        attention_kernel,
        out_shape=jax.ShapeDtypeStruct(sent.shape, jnp.bfloat16),
        in_specs=[smem, smem, vmem],
        out_specs=vmem,
        scratch_shapes=[
            pltpu.VMEM((rows, FEATURES), jnp.bfloat16),
            pltpu.VMEM((keys, rows), jnp.float32),
            pltpu.VMEM((keys, QPK * rows), jnp.bfloat16),
            pltpu.VMEM((keys, QPK * rows), jnp.bfloat16),
        ],
        compiler_params=roomy,
        cost_estimate=pl.CostEstimate(
            flops=10 * rows * keys * HD * QPK, bytes_accessed=4 * sent.size, transcendentals=rows * keys * QPK
        ),
    )(begins, first, sent)


def split_kernel(core_ref, x_ref, keep_ref, send_ref):
    core = core_ref[0]
    tokens = x_ref.shape[0]
    for group in range(16):
        y, zl = divmod(group, 4)
        turned = x_ref[:, group * 256:(group + 1) * 256].astype(jnp.float32).T.reshape(16, 16, tokens)
        lower = turned[:, :8].reshape(128, tokens)
        upper = turned[:, 8:].reshape(128, tokens)
        keep = jnp.where(core == 0, lower, upper).astype(jnp.bfloat16)
        send = jnp.where(core == 0, upper, lower).astype(jnp.bfloat16)
        for x in range(4):
            at = (y * 4 + x) * 128 + zl * 32
            keep_ref[at:at + 32, :] = keep[x * 32:(x + 1) * 32]
            send_ref[at:at + 32, :] = send[x * 32:(x + 1) * 32]


def split_features(core, inputs):
    rows, width = inputs.shape
    shape = jax.ShapeDtypeStruct((width // 2, rows), jnp.bfloat16)
    return pl.pallas_call(
        split_kernel,
        out_shape=(shape, shape),
        in_specs=[smem, vmem],
        out_specs=(vmem, vmem),
        compiler_params=roomy,
        cost_estimate=pl.CostEstimate(flops=4 * inputs.size, bytes_accessed=4 * inputs.size, transcendentals=0),
    )(core, inputs)


def pack_kernel(q_ref, g_ref, mine_ref, other_ref, sent_ref):
    sent_ref[:, :, :WIDTH] = q_ref[...].reshape(COLS, OWN, WIDTH)
    sent_ref[:, :, WIDTH:2 * WIDTH] = g_ref[...].reshape(COLS, OWN, WIDTH)
    kv = (mine_ref[...] + other_ref[...]).astype(jnp.bfloat16).reshape(COLS, OWN, 2 * HD)
    for k in range(BLOCKS):
        back = BLOCKS - 1 - k
        at = 2 * WIDTH + 2 * k * HD
        if back:
            sent_ref[:back, :, at:at + 2 * HD] = jnp.zeros((back, OWN, 2 * HD), jnp.bfloat16)
        sent_ref[back:, :, at:at + 2 * HD] = kv[:COLS - back]


def pack(queries, grads, mine, other):
    return pl.pallas_call(
        pack_kernel,
        out_shape=jax.ShapeDtypeStruct((COLS, OWN, FEATURES), jnp.bfloat16),
        in_specs=[vmem] * 4,
        out_specs=vmem,
        compiler_params=roomy,
        cost_estimate=pl.CostEstimate(flops=mine.size, bytes_accessed=8 * queries.size, transcendentals=0),
    )(queries, grads, mine, other)


def fold_kernel(back_ref, dkv_ref):
    def part(k):
        at = 2 * WIDTH + 2 * k * HD
        return back_ref[:, :, at:at + 2 * HD].astype(jnp.float32)

    total = part(BLOCKS - 1)
    for k in range(1, BLOCKS):
        fill = jnp.zeros((k, OWN, 2 * HD), jnp.float32)
        total = total + jnp.concatenate([part(BLOCKS - 1 - k)[k:], fill], axis=0)
    dkv_ref[...] = total.reshape(COLS * OWN, 2 * HD).astype(jnp.bfloat16)


def fold(back):
    return pl.pallas_call(
        fold_kernel,
        out_shape=jax.ShapeDtypeStruct((COLS * OWN, 2 * HD), jnp.bfloat16),
        in_specs=[vmem],
        out_specs=vmem,
        compiler_params=roomy,
        cost_estimate=pl.CostEstimate(flops=back.size, bytes_accessed=back.size, transcendentals=0),
    )(back)


def weight_kernel(keep_ref, recv_ref, mine_ref, other_ref, out_ref):
    for at in range(0, keep_ref.shape[0], 256):
        rows = slice(at, at + 256)
        total = lax.dot_general(keep_ref[rows], mine_ref[...], plain_dims, preferred_element_type=jnp.float32)
        total += lax.dot_general(recv_ref[rows], other_ref[...], plain_dims, preferred_element_type=jnp.float32)
        out_ref[rows] = total.astype(out_ref.dtype)


def weight_part(keep, recv, mine, other):
    return pl.pallas_call(
        weight_kernel,
        out_shape=jax.ShapeDtypeStruct((keep.shape[0], 2 * HD), jnp.bfloat16),
        in_specs=[vmem] * 4,
        out_specs=vmem,
        compiler_params=roomy,
        cost_estimate=pl.CostEstimate(flops=8 * keep.size * HD, bytes_accessed=6 * keep.size, transcendentals=0),
    )(keep, recv, mine, other)


def exchange(array, axes):
    return lax.all_to_all(array, axes, split_axis=0, concat_axis=0, tiled=True)


def spread(array, axes):
    count = lax.axis_size(axes)
    return exchange(jnp.broadcast_to(array[None], (count,) + array.shape), axes)


def swap(array):
    return lax.ppermute(array, "core", [(0, 1), (1, 0)])


def per_device(layer_input, queries, grad_out, key_weight, value_weight, doc_len):
    inputs = layer_input[0]
    core = lax.axis_index("core").astype(jnp.int32).reshape(1)
    place = lax.axis_index(CTX)
    ends = jnp.cumsum(doc_len[0])
    units = place * OWN + jnp.arange(OWN, dtype=jnp.int32)
    begins = jnp.max(jnp.where(ends[None, :] <= units[:, None], ends[None, :], 0), axis=1)
    first = (place * OWN).astype(jnp.int32).reshape(1)

    keep, send = split_features(core, inputs)
    line = spread(jnp.concatenate([key_weight, value_weight], axis=1), LINE)
    line, keep, send, begins, first = lax.optimization_barrier((line, keep, send, begins, first))
    recv = swap(send)
    weight = spread(line, PLANE).reshape(keep.shape[0], 2 * HD)

    other = lax.dot_general(recv, weight, first_dims, preferred_element_type=jnp.float32)
    other = swap(other)
    mine = lax.dot_general(keep, weight, first_dims, preferred_element_type=jnp.float32)

    sent = exchange(pack(queries[0], grad_out[0], mine, other), CTX)
    back = exchange(attention(begins, first, sent), CTX)

    dkv = fold(back)
    part = weight_part(keep, recv, dkv, swap(dkv)).reshape(16, -1, 2 * HD)
    plane = jnp.sum(exchange(part, PLANE).astype(jnp.float32), axis=0).reshape(16, -1, 2 * HD)
    share = jnp.sum(exchange(plane, LINE), axis=0)

    rows = back.reshape(COLS * OWN, FEATURES)
    return (rows[None, :, :WIDTH], rows[None, :, WIDTH:2 * WIDTH], share[:, :HD], share[:, HD:])


def solution(mesh):
    split = Mesh(mesh.devices.reshape(4, 4, 4, 4, 2), SPLIT)
    isl = ("zh", "core")
    placed = (
        P(isl, CTX, None),
        P(isl, CTX, None),
        P(isl, CTX, None),
        P(SPLIT, None),
        P(SPLIT, None),
        P(isl, None),
    )
    return jax.shard_map(
        per_device,
        mesh=split,
        in_specs=placed,
        out_specs=(
            P(isl, CTX, None),
            P(isl, CTX, None),
            P(SPLIT, None),
            P(SPLIT, None),
        ),
        check_vma=False,
    )
```

```python
import math

import jax
import jax.numpy as jnp
from jax import lax
from jax.experimental import pallas as pl
from jax.experimental.pallas import tpu as pltpu
from jax.sharding import Mesh, PartitionSpec as P

HD = 128
QPK = 8
WIDTH = QPK * HD
COLS = 64
OWN = 4
BLOCKS = 3

SPLIT = ("y", "zl", "x", "zh", "core")
CTX = ("y", "zl", "x")
PLANE = ("y", "x")
LINE = ("zl", "zh")
last_dims = (((1,), (1,)), ((), ()))
plain_dims = (((1,), (0,)), ((), ()))
first_dims = (((0,), (0,)), ((), ()))
hidden = -1e30
FEATURES = 2 * WIDTH + 2 * BLOCKS * HD
vmem = pl.BlockSpec(memory_space=pltpu.VMEM)
smem = pl.BlockSpec(memory_space=pltpu.SMEM)
roomy = pltpu.CompilerParams(vmem_limit_bytes=40 * 1024 * 1024)


def attention_kernel(begin_ref, first_ref, sent_ref, back_ref, got_ref, bias_ref, dkey_ref, dvalue_ref):
    rows = COLS * OWN
    keys = BLOCKS * rows
    first = first_ref[0]
    got_ref[...] = sent_ref[...].reshape(rows, FEATURES)
    scale = float(HD) ** -0.5
    factor = scale * math.log2(math.e)

    key_row = lax.broadcasted_iota(jnp.int32, (keys, 1), 0)
    key_block = key_row // rows
    key_col = (key_row - key_block * rows) // OWN
    key_unit = first + (key_block - (BLOCKS - 1)) * OWN + key_row % OWN
    key_pos = key_unit * COLS + key_col
    row = lax.broadcasted_iota(jnp.int32, (1, rows), 1)
    slot = row % OWN
    row_pos = (first + slot) * COLS + row // OWN
    start = jnp.zeros((1, rows), jnp.int32)
    for i in range(OWN):
        start = jnp.where(slot == i, begin_ref[i], start)
    allowed = (key_unit >= start) & (key_pos <= row_pos)
    bias_ref[...] = jnp.where(allowed, 0.0, hidden).astype(jnp.float32)

    def window(place):
        parts = [got_ref[:, 2 * WIDTH + (2 * k + place) * HD:][:, :HD] for k in range(BLOCKS)]
        return jnp.concatenate(parts, axis=0)

    key, value = window(0), window(1)
    key_t, value_t = key.T, value.T
    held = {}

    def query(head):
        return got_ref[:, head * HD:(head + 1) * HD]

    def grad(head):
        return got_ref[:, WIDTH + head * HD:WIDTH + (head + 1) * HD]

    def put(at, block):
        back_ref[:, :, at:at + HD] = block.astype(jnp.bfloat16).reshape(COLS, OWN, HD)

    def add(ref, head, term):
        if head:
            ref[...] += term
        else:
            ref[...] = term

    def score(head):
        held["score", head] = lax.dot_general(key, query(head), last_dims, preferred_element_type=jnp.float32)

    def softmax(head):
        scaled = held.pop(("score", head)) * factor + bias_ref[...]
        expo = jnp.exp2(scaled - jnp.max(scaled, axis=0, keepdims=True))
        held["probs", head] = expo * (1.0 / jnp.sum(expo, axis=0, keepdims=True))
        held["low", head] = held["probs", head].astype(jnp.bfloat16)

    def dvalues(head):
        add(dvalue_ref, head, lax.dot_general(held.pop(("low", head)), grad(head), plain_dims, preferred_element_type=jnp.float32))

    def dprobs(head):
        held["dprobs", head] = lax.dot_general(value, grad(head), last_dims, preferred_element_type=jnp.float32)

    def output(head):
        out_t = lax.dot_general(value_t, held["low", head], plain_dims, preferred_element_type=jnp.float32).astype(jnp.bfloat16)
        put(head * HD, out_t.T)
        product = grad(head).T.astype(jnp.float32) * out_t.astype(jnp.float32)
        held["delta", head] = jnp.sum(product, axis=0, keepdims=True)

    def dscores(head):
        difference = held.pop(("dprobs", head)) - held.pop(("delta", head))
        held["dscores", head] = (held.pop(("probs", head)) * difference).astype(jnp.bfloat16)

    def dqueries(head):
        dscore = held.pop(("dscores", head))
        dquery_t = lax.dot_general(key_t, dscore, plain_dims, preferred_element_type=jnp.float32) * scale
        put(WIDTH + head * HD, dquery_t.astype(jnp.bfloat16).T)
        add(dkey_ref, head, lax.dot_general(dscore, query(head), plain_dims, preferred_element_type=jnp.float32))

    order = ((score, 0), (softmax, 1), (dvalues, 2), (dprobs, 1), (output, 1), (dqueries, 2), (dscores, 1))
    for turn in range(QPK + 2):
        for step, lag in order:
            if 0 <= turn - lag < QPK:
                step(turn - lag)
    for k in range(BLOCKS):
        block = slice(k * rows, (k + 1) * rows)
        put(2 * WIDTH + 2 * k * HD, dkey_ref[block] * scale)
        put(2 * WIDTH + (2 * k + 1) * HD, dvalue_ref[block])


def attention(begins, first, sent):
    rows = COLS * OWN
    keys = BLOCKS * rows
    return pl.pallas_call(
        attention_kernel,
        out_shape=jax.ShapeDtypeStruct(sent.shape, jnp.bfloat16),
        in_specs=[smem, smem, vmem],
        out_specs=vmem,
        scratch_shapes=[
            pltpu.VMEM((rows, FEATURES), jnp.bfloat16),
            pltpu.VMEM((keys, rows), jnp.float32),
            pltpu.VMEM((keys, HD), jnp.float32),
            pltpu.VMEM((keys, HD), jnp.float32),
        ],
        compiler_params=roomy,
        cost_estimate=pl.CostEstimate(
            flops=10 * rows * keys * HD * QPK, bytes_accessed=4 * sent.size, transcendentals=rows * keys * QPK
        ),
    )(begins, first, sent)


def split_kernel(core_ref, x_ref, keep_ref, send_ref):
    core = core_ref[0]
    tokens = x_ref.shape[0]
    for group in range(16):
        y, zl = divmod(group, 4)
        turned = x_ref[:, group * 256:(group + 1) * 256].astype(jnp.float32).T.reshape(16, 16, tokens)
        lower = turned[:, :8].reshape(128, tokens)
        upper = turned[:, 8:].reshape(128, tokens)
        keep = jnp.where(core == 0, lower, upper).astype(jnp.bfloat16)
        send = jnp.where(core == 0, upper, lower).astype(jnp.bfloat16)
        for x in range(4):
            at = (y * 4 + x) * 128 + zl * 32
            keep_ref[at:at + 32, :] = keep[x * 32:(x + 1) * 32]
            send_ref[at:at + 32, :] = send[x * 32:(x + 1) * 32]


def split_features(core, inputs):
    rows, width = inputs.shape
    shape = jax.ShapeDtypeStruct((width // 2, rows), jnp.bfloat16)
    return pl.pallas_call(
        split_kernel,
        out_shape=(shape, shape),
        in_specs=[smem, vmem],
        out_specs=(vmem, vmem),
        compiler_params=roomy,
        cost_estimate=pl.CostEstimate(flops=4 * inputs.size, bytes_accessed=4 * inputs.size, transcendentals=0),
    )(core, inputs)


def pack_kernel(q_ref, g_ref, mine_ref, other_ref, sent_ref):
    sent_ref[:, :, :WIDTH] = q_ref[...].reshape(COLS, OWN, WIDTH)
    sent_ref[:, :, WIDTH:2 * WIDTH] = g_ref[...].reshape(COLS, OWN, WIDTH)
    kv = (mine_ref[...] + other_ref[...]).astype(jnp.bfloat16).reshape(COLS, OWN, 2 * HD)
    for k in range(BLOCKS):
        back = BLOCKS - 1 - k
        at = 2 * WIDTH + 2 * k * HD
        if back:
            sent_ref[:back, :, at:at + 2 * HD] = jnp.zeros((back, OWN, 2 * HD), jnp.bfloat16)
        sent_ref[back:, :, at:at + 2 * HD] = kv[:COLS - back]


def pack(queries, grads, mine, other):
    return pl.pallas_call(
        pack_kernel,
        out_shape=jax.ShapeDtypeStruct((COLS, OWN, FEATURES), jnp.bfloat16),
        in_specs=[vmem] * 4,
        out_specs=vmem,
        compiler_params=roomy,
        cost_estimate=pl.CostEstimate(flops=mine.size, bytes_accessed=8 * queries.size, transcendentals=0),
    )(queries, grads, mine, other)


def fold_kernel(back_ref, dkv_ref):
    def part(k):
        at = 2 * WIDTH + 2 * k * HD
        return back_ref[:, :, at:at + 2 * HD].astype(jnp.float32)

    total = part(BLOCKS - 1)
    for k in range(1, BLOCKS):
        fill = jnp.zeros((k, OWN, 2 * HD), jnp.float32)
        total = total + jnp.concatenate([part(BLOCKS - 1 - k)[k:], fill], axis=0)
    dkv_ref[...] = total.reshape(COLS * OWN, 2 * HD).astype(jnp.bfloat16)


def fold(back):
    return pl.pallas_call(
        fold_kernel,
        out_shape=jax.ShapeDtypeStruct((COLS * OWN, 2 * HD), jnp.bfloat16),
        in_specs=[vmem],
        out_specs=vmem,
        compiler_params=roomy,
        cost_estimate=pl.CostEstimate(flops=back.size, bytes_accessed=back.size, transcendentals=0),
    )(back)


def weight_kernel(keep_ref, recv_ref, mine_ref, other_ref, out_ref):
    for at in range(0, keep_ref.shape[0], 256):
        rows = slice(at, at + 256)
        total = lax.dot_general(keep_ref[rows], mine_ref[...], plain_dims, preferred_element_type=jnp.float32)
        total += lax.dot_general(recv_ref[rows], other_ref[...], plain_dims, preferred_element_type=jnp.float32)
        out_ref[rows] = total.astype(out_ref.dtype)


def weight_part(keep, recv, mine, other):
    return pl.pallas_call(
        weight_kernel,
        out_shape=jax.ShapeDtypeStruct((keep.shape[0], 2 * HD), jnp.bfloat16),
        in_specs=[vmem] * 4,
        out_specs=vmem,
        compiler_params=roomy,
        cost_estimate=pl.CostEstimate(flops=8 * keep.size * HD, bytes_accessed=6 * keep.size, transcendentals=0),
    )(keep, recv, mine, other)


def exchange(array, axes):
    return lax.all_to_all(array, axes, split_axis=0, concat_axis=0, tiled=True)


def spread(array, axes):
    count = lax.axis_size(axes)
    return exchange(jnp.broadcast_to(array[None], (count,) + array.shape), axes)


def copies_kernel(key_ref, value_ref, out_ref):
    out_ref[:, :, :HD] = jnp.broadcast_to(key_ref[...][None], out_ref.shape[:2] + (HD,))
    out_ref[:, :, HD:] = jnp.broadcast_to(value_ref[...][None], out_ref.shape[:2] + (HD,))


def weight_copies(key_weight, value_weight, count):
    rows = key_weight.shape[0]
    return pl.pallas_call(
        copies_kernel,
        out_shape=jax.ShapeDtypeStruct((count, rows, 2 * HD), jnp.bfloat16),
        in_specs=[vmem] * 2,
        out_specs=vmem,
        cost_estimate=pl.CostEstimate(flops=0, bytes_accessed=4 * count * rows * HD, transcendentals=0),
    )(key_weight, value_weight)


def swap(array):
    return lax.ppermute(array, "core", [(0, 1), (1, 0)])


def per_device(layer_input, queries, grad_out, key_weight, value_weight, doc_len):
    inputs = layer_input[0]
    core = lax.axis_index("core").astype(jnp.int32).reshape(1)
    place = lax.axis_index(CTX)
    ends = jnp.cumsum(doc_len[0])
    units = place * OWN + jnp.arange(OWN, dtype=jnp.int32)
    begins = jnp.max(jnp.where(ends[None, :] <= units[:, None], ends[None, :], 0), axis=1)
    first = (place * OWN).astype(jnp.int32).reshape(1)

    keep, send = split_features(core, inputs)
    line = exchange(weight_copies(key_weight, value_weight, 16), LINE)
    line, keep, send, begins, first = lax.optimization_barrier((line, keep, send, begins, first))
    recv = swap(send)
    weight = spread(line, PLANE).reshape(keep.shape[0], 2 * HD)

    other = lax.dot_general(recv, weight, first_dims, preferred_element_type=jnp.float32)
    other = swap(other)
    mine = lax.dot_general(keep, weight, first_dims, preferred_element_type=jnp.float32)

    sent = exchange(pack(queries[0], grad_out[0], mine, other), CTX)
    back = exchange(attention(begins, first, sent), CTX)

    dkv = fold(back)
    part = weight_part(keep, recv, dkv, swap(dkv)).reshape(16, -1, 2 * HD)
    plane = jnp.sum(exchange(part, PLANE).astype(jnp.float32), axis=0).reshape(16, -1, 2 * HD)
    share = jnp.sum(exchange(plane, LINE), axis=0)

    rows = back.reshape(COLS * OWN, FEATURES)
    return (rows[None, :, :WIDTH], rows[None, :, WIDTH:2 * WIDTH], share[:, :HD], share[:, HD:])


def solution(mesh):
    split = Mesh(mesh.devices.reshape(4, 4, 4, 4, 2), SPLIT)
    isl = ("zh", "core")
    placed = (
        P(isl, CTX, None),
        P(isl, CTX, None),
        P(isl, CTX, None),
        P(SPLIT, None),
        P(SPLIT, None),
        P(isl, None),
    )
    return jax.shard_map(
        per_device,
        mesh=split,
        in_specs=placed,
        out_specs=(
            P(isl, CTX, None),
            P(isl, CTX, None),
            P(SPLIT, None),
            P(SPLIT, None),
        ),
        check_vma=False,
    )
```

```python
import math

import jax
import jax.numpy as jnp
from jax import lax
from jax.experimental import pallas as pl
from jax.experimental.pallas import tpu as pltpu
from jax.sharding import Mesh, PartitionSpec as P

HD = 128
QPK = 8
WIDTH = QPK * HD
COLS = 64
OWN = 4
BLOCKS = 3

SPLIT = ("y", "zl", "x", "zh", "core")
CTX = ("y", "zl", "x")
PEERS = ("zl", "x", "y")
PLANE = ("x", "y")
LINE = ("zl", "zh")
last_dims = (((1,), (1,)), ((), ()))
plain_dims = (((1,), (0,)), ((), ()))
first_dims = (((0,), (0,)), ((), ()))
hidden = -1e30
FEATURES = 2 * WIDTH + 2 * BLOCKS * HD
vmem = pl.BlockSpec(memory_space=pltpu.VMEM)
smem = pl.BlockSpec(memory_space=pltpu.SMEM)
roomy = pltpu.CompilerParams(vmem_limit_bytes=40 * 1024 * 1024)


def column_of(peer):
    return (peer % 4) * 16 + (peer // 16) * 4 + peer // 4 % 4


def attention_kernel(begin_ref, first_ref, sent_ref, back_ref, got_ref, bias_ref, dkey_ref, dvalue_ref):
    rows = COLS * OWN
    keys = BLOCKS * rows
    first = first_ref[0]
    got_ref[...] = sent_ref[...].reshape(rows, FEATURES)
    scale = float(HD) ** -0.5
    factor = scale * math.log2(math.e)

    key_row = lax.broadcasted_iota(jnp.int32, (keys, 1), 0)
    key_block = key_row // rows
    key_col = column_of((key_row - key_block * rows) // OWN)
    key_unit = first + (key_block - (BLOCKS - 1)) * OWN + key_row % OWN
    key_pos = key_unit * COLS + key_col
    row = lax.broadcasted_iota(jnp.int32, (1, rows), 1)
    slot = row % OWN
    row_pos = (first + slot) * COLS + column_of(row // OWN)
    start = jnp.zeros((1, rows), jnp.int32)
    for i in range(OWN):
        start = jnp.where(slot == i, begin_ref[i], start)
    allowed = (key_unit >= start) & (key_pos <= row_pos)
    bias_ref[...] = jnp.where(allowed, 0.0, hidden).astype(jnp.float32)

    def window(place):
        parts = [got_ref[:, 2 * WIDTH + (2 * k + place) * HD:][:, :HD] for k in range(BLOCKS)]
        return jnp.concatenate(parts, axis=0)

    key, value = window(0), window(1)
    key_t, value_t = key.T, value.T
    held = {}

    def query(head):
        return got_ref[:, head * HD:(head + 1) * HD]

    def grad(head):
        return got_ref[:, WIDTH + head * HD:WIDTH + (head + 1) * HD]

    def put(at, block):
        back_ref[:, :, at:at + HD] = block.astype(jnp.bfloat16).reshape(COLS, OWN, HD)

    def add(ref, head, term):
        if head:
            ref[...] += term
        else:
            ref[...] = term

    def score(head):
        held["score", head] = lax.dot_general(key, query(head), last_dims, preferred_element_type=jnp.float32)

    def softmax(head):
        scaled = held.pop(("score", head)) * factor + bias_ref[...]
        expo = jnp.exp2(scaled - jnp.max(scaled, axis=0, keepdims=True))
        held["probs", head] = expo * (1.0 / jnp.sum(expo, axis=0, keepdims=True))
        held["low", head] = held["probs", head].astype(jnp.bfloat16)

    def dvalues(head):
        add(dvalue_ref, head, lax.dot_general(held.pop(("low", head)), grad(head), plain_dims, preferred_element_type=jnp.float32))

    def dprobs(head):
        held["dprobs", head] = lax.dot_general(value, grad(head), last_dims, preferred_element_type=jnp.float32)

    def output(head):
        out_t = lax.dot_general(value_t, held["low", head], plain_dims, preferred_element_type=jnp.float32).astype(jnp.bfloat16)
        put(head * HD, out_t.T)
        product = grad(head).T.astype(jnp.float32) * out_t.astype(jnp.float32)
        held["delta", head] = jnp.sum(product, axis=0, keepdims=True)

    def dscores(head):
        difference = held.pop(("dprobs", head)) - held.pop(("delta", head))
        held["dscores", head] = (held.pop(("probs", head)) * difference).astype(jnp.bfloat16)

    def dqueries(head):
        dscore = held.pop(("dscores", head))
        dquery_t = lax.dot_general(key_t, dscore, plain_dims, preferred_element_type=jnp.float32) * scale
        put(WIDTH + head * HD, dquery_t.astype(jnp.bfloat16).T)
        add(dkey_ref, head, lax.dot_general(dscore, query(head), plain_dims, preferred_element_type=jnp.float32))

    order = ((score, 0), (softmax, 1), (dvalues, 2), (dprobs, 1), (output, 1), (dqueries, 2), (dscores, 1))
    for turn in range(QPK + 2):
        for step, lag in order:
            if 0 <= turn - lag < QPK:
                step(turn - lag)
    for k in range(BLOCKS):
        block = slice(k * rows, (k + 1) * rows)
        put(2 * WIDTH + 2 * k * HD, dkey_ref[block] * scale)
        put(2 * WIDTH + (2 * k + 1) * HD, dvalue_ref[block])


def attention(begins, first, sent):
    rows = COLS * OWN
    keys = BLOCKS * rows
    return pl.pallas_call(
        attention_kernel,
        out_shape=jax.ShapeDtypeStruct(sent.shape, jnp.bfloat16),
        in_specs=[smem, smem, vmem],
        out_specs=vmem,
        scratch_shapes=[
            pltpu.VMEM((rows, FEATURES), jnp.bfloat16),
            pltpu.VMEM((keys, rows), jnp.float32),
            pltpu.VMEM((keys, HD), jnp.float32),
            pltpu.VMEM((keys, HD), jnp.float32),
        ],
        compiler_params=roomy,
        cost_estimate=pl.CostEstimate(
            flops=10 * rows * keys * HD * QPK, bytes_accessed=4 * sent.size, transcendentals=rows * keys * QPK
        ),
    )(begins, first, sent)


def split_kernel(core_ref, x_ref, keep_ref, send_ref):
    core = core_ref[0]
    tokens = x_ref.shape[0]
    for group in range(16):
        y, zl = divmod(group, 4)
        turned = x_ref[:, group * 256:(group + 1) * 256].astype(jnp.float32).T.reshape(16, 16, tokens)
        lower = turned[:, :8].reshape(128, tokens)
        upper = turned[:, 8:].reshape(128, tokens)
        keep = jnp.where(core == 0, lower, upper).astype(jnp.bfloat16)
        send = jnp.where(core == 0, upper, lower).astype(jnp.bfloat16)
        for x in range(4):
            at = (x * 4 + y) * 128 + zl * 32
            keep_ref[at:at + 32, :] = keep[x * 32:(x + 1) * 32]
            send_ref[at:at + 32, :] = send[x * 32:(x + 1) * 32]


def split_features(core, inputs):
    rows, width = inputs.shape
    shape = jax.ShapeDtypeStruct((width // 2, rows), jnp.bfloat16)
    return pl.pallas_call(
        split_kernel,
        out_shape=(shape, shape),
        in_specs=[smem, vmem],
        out_specs=(vmem, vmem),
        compiler_params=roomy,
        cost_estimate=pl.CostEstimate(flops=4 * inputs.size, bytes_accessed=4 * inputs.size, transcendentals=0),
    )(core, inputs)


def pack_kernel(q_ref, g_ref, mine_ref, other_ref, sent_ref):
    sent_ref[:, :, :WIDTH] = q_ref[...].reshape(COLS, OWN, WIDTH)
    sent_ref[:, :, WIDTH:2 * WIDTH] = g_ref[...].reshape(COLS, OWN, WIDTH)
    kv = (mine_ref[...] + other_ref[...]).astype(jnp.bfloat16).reshape(COLS, OWN, 2 * HD)
    for k in range(BLOCKS):
        back = BLOCKS - 1 - k
        at = 2 * WIDTH + 2 * k * HD
        if back:
            sent_ref[:back, :, at:at + 2 * HD] = jnp.zeros((back, OWN, 2 * HD), jnp.bfloat16)
        sent_ref[back:, :, at:at + 2 * HD] = kv[:COLS - back]


def pack(queries, grads, mine, other):
    return pl.pallas_call(
        pack_kernel,
        out_shape=jax.ShapeDtypeStruct((COLS, OWN, FEATURES), jnp.bfloat16),
        in_specs=[vmem] * 4,
        out_specs=vmem,
        compiler_params=roomy,
        cost_estimate=pl.CostEstimate(flops=mine.size, bytes_accessed=8 * queries.size, transcendentals=0),
    )(queries, grads, mine, other)


def fold_kernel(back_ref, dkv_ref):
    def part(k):
        at = 2 * WIDTH + 2 * k * HD
        return back_ref[:, :, at:at + 2 * HD].astype(jnp.float32)

    total = part(BLOCKS - 1)
    for k in range(1, BLOCKS):
        fill = jnp.zeros((k, OWN, 2 * HD), jnp.float32)
        total = total + jnp.concatenate([part(BLOCKS - 1 - k)[k:], fill], axis=0)
    dkv_ref[...] = total.reshape(COLS * OWN, 2 * HD).astype(jnp.bfloat16)


def fold(back):
    return pl.pallas_call(
        fold_kernel,
        out_shape=jax.ShapeDtypeStruct((COLS * OWN, 2 * HD), jnp.bfloat16),
        in_specs=[vmem],
        out_specs=vmem,
        compiler_params=roomy,
        cost_estimate=pl.CostEstimate(flops=back.size, bytes_accessed=back.size, transcendentals=0),
    )(back)


def exchange(array, axes):
    return lax.all_to_all(array, axes, split_axis=0, concat_axis=0, tiled=True)


def spread(array, axes):
    count = lax.axis_size(axes)
    return exchange(jnp.broadcast_to(array[None], (count,) + array.shape), axes)


def swap(array):
    return lax.ppermute(array, "core", [(0, 1), (1, 0)])


def per_device(layer_input, queries, grad_out, key_weight, value_weight, doc_len):
    inputs = layer_input[0]
    core = lax.axis_index("core").astype(jnp.int32).reshape(1)
    place = lax.axis_index(PEERS)
    ends = jnp.cumsum(doc_len[0])
    units = place * OWN + jnp.arange(OWN, dtype=jnp.int32)
    begins = jnp.max(jnp.where(ends[None, :] <= units[:, None], ends[None, :], 0), axis=1)
    first = (place * OWN).astype(jnp.int32).reshape(1)

    line = spread(jnp.concatenate([key_weight, value_weight], axis=1), LINE)
    keep, send = split_features(core, inputs)
    line, keep, send, begins, first = lax.optimization_barrier((line, keep, send, begins, first))
    weight = spread(line, PLANE).reshape(keep.shape[0], 2 * HD)

    other = lax.dot_general(send, swap(weight), first_dims, preferred_element_type=jnp.float32)
    mine = lax.dot_general(keep, weight, first_dims, preferred_element_type=jnp.float32)

    sent = exchange(pack(queries[0], grad_out[0], mine, other), PEERS)
    back = exchange(attention(begins, first, sent), PEERS)

    dkv = fold(back)
    away = jnp.dot(send, dkv, preferred_element_type=jnp.float32).astype(jnp.bfloat16)
    part = jnp.dot(keep, dkv, preferred_element_type=jnp.float32) + swap(away).astype(jnp.float32)
    part = part.astype(jnp.bfloat16).reshape(16, -1, 2 * HD)
    plane = jnp.sum(exchange(part, PLANE).astype(jnp.float32), axis=0).reshape(16, -1, 2 * HD)
    share = jnp.sum(exchange(plane, LINE), axis=0)

    rows = back.reshape(COLS * OWN, FEATURES)
    return (rows[None, :, :WIDTH], rows[None, :, WIDTH:2 * WIDTH], share[:, :HD], share[:, HD:])


def solution(mesh):
    split = Mesh(mesh.devices.reshape(4, 4, 4, 4, 2), SPLIT)
    isl = ("zh", "core")
    placed = (
        P(isl, CTX, None),
        P(isl, CTX, None),
        P(isl, CTX, None),
        P(SPLIT, None),
        P(SPLIT, None),
        P(isl, None),
    )
    return jax.shard_map(
        per_device,
        mesh=split,
        in_specs=placed,
        out_specs=(
            P(isl, CTX, None),
            P(isl, CTX, None),
            P(SPLIT, None),
            P(SPLIT, None),
        ),
        check_vma=False,
    )
```

```python
import math

import jax
import jax.numpy as jnp
from jax import lax
from jax.experimental import pallas as pl
from jax.experimental.pallas import tpu as pltpu
from jax.sharding import Mesh, PartitionSpec as P

HD = 128
QPK = 8
WIDTH = QPK * HD
COLS = 64
OWN = 4
BLOCKS = 3

SPLIT = ("y", "zl", "x", "zh", "core")
CTX = ("y", "zl", "x")
PEERS = ("zl", "x", "y")
PLANE = ("x", "y")
LINE = ("zl", "zh")
last_dims = (((1,), (1,)), ((), ()))
plain_dims = (((1,), (0,)), ((), ()))
first_dims = (((0,), (0,)), ((), ()))
hidden = -1e30
FEATURES = 2 * WIDTH + 2 * BLOCKS * HD
vmem = pl.BlockSpec(memory_space=pltpu.VMEM)
smem = pl.BlockSpec(memory_space=pltpu.SMEM)
roomy = pltpu.CompilerParams(vmem_limit_bytes=40 * 1024 * 1024)


def attention_kernel(begin_ref, first_ref, sent_ref, back_ref, got_ref, bias_ref, dkey_ref, dvalue_ref):
    rows = COLS * OWN
    keys = BLOCKS * rows
    first = first_ref[0]
    got_ref[...] = sent_ref[...].reshape(rows, FEATURES)
    scale = float(HD) ** -0.5
    factor = scale * math.log2(math.e)

    def position(row):
        return ((row & 3) << 6) + (((row >> 2) & 3) << 4) + ((row >> 6) << 2) + ((row >> 4) & 3)

    row = lax.broadcasted_iota(jnp.int32, (1, rows), 1)
    start = jnp.zeros((1, rows), jnp.int32)
    for i in range(OWN):
        start = jnp.where((row & 3) == i, (begin_ref[i] - first) * COLS, start)
    key_pos = position(lax.broadcasted_iota(jnp.int32, (rows, 1), 0))
    for k in range(BLOCKS):
        shifted = key_pos - (BLOCKS - 1 - k) * OWN * COLS
        allowed = shifted >= start
        if k == BLOCKS - 1:
            allowed = allowed & (shifted <= position(row))
        bias_ref[k * rows:(k + 1) * rows] = jnp.where(allowed, 0.0, hidden).astype(jnp.float32)

    def window(place):
        parts = [got_ref[:, 2 * WIDTH + (2 * k + place) * HD:][:, :HD] for k in range(BLOCKS)]
        return jnp.concatenate(parts, axis=0)

    key, value = window(0), window(1)
    key_t, value_t = key.T, value.T
    held = {}

    def query(head):
        return got_ref[:, head * HD:(head + 1) * HD]

    def grad(head):
        return got_ref[:, WIDTH + head * HD:WIDTH + (head + 1) * HD]

    def put(at, block):
        back_ref[:, :, at:at + HD] = block.astype(jnp.bfloat16).reshape(COLS, OWN, HD)

    def add(ref, head, term):
        if head:
            ref[...] += term
        else:
            ref[...] = term

    def score(head):
        held["score", head] = lax.dot_general(key, query(head), last_dims, preferred_element_type=jnp.float32)

    def softmax(head):
        scaled = held.pop(("score", head)) * factor + bias_ref[...]
        expo = jnp.exp2(scaled - jnp.max(scaled, axis=0, keepdims=True))
        held["probs", head] = expo * (1.0 / jnp.sum(expo, axis=0, keepdims=True))
        held["low", head] = held["probs", head].astype(jnp.bfloat16)

    def dvalues(head):
        add(dvalue_ref, head, lax.dot_general(held.pop(("low", head)), grad(head), plain_dims, preferred_element_type=jnp.float32))

    def dprobs(head):
        held["dprobs", head] = lax.dot_general(value, grad(head), last_dims, preferred_element_type=jnp.float32)

    def output(head):
        out_t = lax.dot_general(value_t, held["low", head], plain_dims, preferred_element_type=jnp.float32).astype(jnp.bfloat16)
        put(head * HD, out_t.T)
        product = grad(head).T.astype(jnp.float32) * out_t.astype(jnp.float32)
        held["delta", head] = jnp.sum(product, axis=0, keepdims=True)

    def dscores(head):
        difference = held.pop(("dprobs", head)) - held.pop(("delta", head))
        held["dscores", head] = (held.pop(("probs", head)) * difference).astype(jnp.bfloat16)

    def dqueries(head):
        dscore = held.pop(("dscores", head))
        dquery_t = lax.dot_general(key_t, dscore, plain_dims, preferred_element_type=jnp.float32) * scale
        put(WIDTH + head * HD, dquery_t.astype(jnp.bfloat16).T)
        add(dkey_ref, head, lax.dot_general(dscore, query(head), plain_dims, preferred_element_type=jnp.float32))

    order = ((score, 0), (softmax, 1), (dvalues, 2), (dprobs, 1), (output, 1), (dqueries, 2), (dscores, 1))
    for turn in range(QPK + 2):
        for step, lag in order:
            if 0 <= turn - lag < QPK:
                step(turn - lag)
    for k in range(BLOCKS):
        block = slice(k * rows, (k + 1) * rows)
        put(2 * WIDTH + 2 * k * HD, dkey_ref[block] * scale)
        put(2 * WIDTH + (2 * k + 1) * HD, dvalue_ref[block])


def attention(begins, first, sent):
    rows = COLS * OWN
    keys = BLOCKS * rows
    return pl.pallas_call(
        attention_kernel,
        out_shape=jax.ShapeDtypeStruct(sent.shape, jnp.bfloat16),
        in_specs=[smem, smem, vmem],
        out_specs=vmem,
        scratch_shapes=[
            pltpu.VMEM((rows, FEATURES), jnp.bfloat16),
            pltpu.VMEM((keys, rows), jnp.float32),
            pltpu.VMEM((keys, HD), jnp.float32),
            pltpu.VMEM((keys, HD), jnp.float32),
        ],
        compiler_params=roomy,
        cost_estimate=pl.CostEstimate(
            flops=10 * rows * keys * HD * QPK, bytes_accessed=4 * sent.size, transcendentals=rows * keys * QPK
        ),
    )(begins, first, sent)


def split_kernel(core_ref, x_ref, keep_ref, send_ref):
    core = core_ref[0]
    tokens = x_ref.shape[0]
    for group in range(16):
        y, zl = divmod(group, 4)
        turned = x_ref[:, group * 256:(group + 1) * 256].astype(jnp.float32).T.reshape(16, 16, tokens)
        lower = turned[:, :8].reshape(128, tokens)
        upper = turned[:, 8:].reshape(128, tokens)
        keep = jnp.where(core == 0, lower, upper).astype(jnp.bfloat16)
        send = jnp.where(core == 0, upper, lower).astype(jnp.bfloat16)
        for x in range(4):
            at = (x * 4 + y) * 128 + zl * 32
            keep_ref[at:at + 32, :] = keep[x * 32:(x + 1) * 32]
            send_ref[at:at + 32, :] = send[x * 32:(x + 1) * 32]


def split_features(core, inputs):
    rows, width = inputs.shape
    shape = jax.ShapeDtypeStruct((width // 2, rows), jnp.bfloat16)
    return pl.pallas_call(
        split_kernel,
        out_shape=(shape, shape),
        in_specs=[smem, vmem],
        out_specs=(vmem, vmem),
        compiler_params=roomy,
        cost_estimate=pl.CostEstimate(flops=4 * inputs.size, bytes_accessed=4 * inputs.size, transcendentals=0),
    )(core, inputs)


def pack_kernel(q_ref, g_ref, mine_ref, other_ref, sent_ref):
    sent_ref[:, :, :WIDTH] = q_ref[...].reshape(COLS, OWN, WIDTH)
    sent_ref[:, :, WIDTH:2 * WIDTH] = g_ref[...].reshape(COLS, OWN, WIDTH)
    kv = (mine_ref[...] + other_ref[...]).astype(jnp.bfloat16).reshape(COLS, OWN, 2 * HD)
    for k in range(BLOCKS):
        back = BLOCKS - 1 - k
        at = 2 * WIDTH + 2 * k * HD
        if back:
            sent_ref[:back, :, at:at + 2 * HD] = jnp.zeros((back, OWN, 2 * HD), jnp.bfloat16)
        sent_ref[back:, :, at:at + 2 * HD] = kv[:COLS - back]


def pack(queries, grads, mine, other):
    return pl.pallas_call(
        pack_kernel,
        out_shape=jax.ShapeDtypeStruct((COLS, OWN, FEATURES), jnp.bfloat16),
        in_specs=[vmem] * 4,
        out_specs=vmem,
        compiler_params=roomy,
        cost_estimate=pl.CostEstimate(flops=mine.size, bytes_accessed=8 * queries.size, transcendentals=0),
    )(queries, grads, mine, other)


def fold_kernel(back_ref, dkv_ref):
    def part(k):
        at = 2 * WIDTH + 2 * k * HD
        return back_ref[:, :, at:at + 2 * HD].astype(jnp.float32)

    total = part(BLOCKS - 1)
    for k in range(1, BLOCKS):
        fill = jnp.zeros((k, OWN, 2 * HD), jnp.float32)
        total = total + jnp.concatenate([part(BLOCKS - 1 - k)[k:], fill], axis=0)
    dkv_ref[...] = total.reshape(COLS * OWN, 2 * HD).astype(jnp.bfloat16)


def fold(back):
    return pl.pallas_call(
        fold_kernel,
        out_shape=jax.ShapeDtypeStruct((COLS * OWN, 2 * HD), jnp.bfloat16),
        in_specs=[vmem],
        out_specs=vmem,
        compiler_params=roomy,
        cost_estimate=pl.CostEstimate(flops=back.size, bytes_accessed=back.size, transcendentals=0),
    )(back)


def exchange(array, axes):
    return lax.all_to_all(array, axes, split_axis=0, concat_axis=0, tiled=True)


def spread(array, axes):
    count = lax.axis_size(axes)
    return exchange(jnp.broadcast_to(array[None], (count,) + array.shape), axes)


def swap(array):
    return lax.ppermute(array, "core", [(0, 1), (1, 0)])


def per_device(layer_input, queries, grad_out, key_weight, value_weight, doc_len):
    inputs = layer_input[0]
    core = lax.axis_index("core").astype(jnp.int32).reshape(1)

    line = spread(jnp.concatenate([key_weight, value_weight], axis=1), LINE)
    keep, send = split_features(core, inputs)
    line, keep, send = lax.optimization_barrier((line, keep, send))
    recv = swap(send)
    weight = spread(line, PLANE).reshape(keep.shape[0], 2 * HD)

    other = lax.dot_general(recv, weight, first_dims, preferred_element_type=jnp.float32)
    other, keep, lengths = lax.optimization_barrier((other, keep, doc_len[0]))
    other = swap(other)
    mine = lax.dot_general(keep, weight, first_dims, preferred_element_type=jnp.float32)

    first = lax.axis_index(PEERS).astype(jnp.int32) * OWN
    units = first + jnp.arange(OWN, dtype=jnp.int32)
    numbers = jnp.arange(lengths.shape[0], dtype=jnp.int32)
    ends = jnp.sum(jnp.where(numbers[None, :] <= numbers[:, None], lengths[None, :], 0), axis=1)
    begins = jnp.max(jnp.where(ends[None, :] <= units[:, None], ends[None, :], 0), axis=1)
    first = first.reshape(1)

    sent = exchange(pack(queries[0], grad_out[0], mine, other), PEERS)
    back = exchange(attention(begins, first, sent), PEERS)

    dkv = fold(back)
    part = jnp.dot(keep, dkv, preferred_element_type=jnp.float32)
    part = part + jnp.dot(recv, swap(dkv), preferred_element_type=jnp.float32)
    part = part.astype(jnp.bfloat16).reshape(16, -1, 2 * HD)
    plane = jnp.sum(exchange(part, PLANE).astype(jnp.float32), axis=0).reshape(16, -1, 2 * HD)
    share = jnp.sum(exchange(plane, LINE), axis=0)

    rows = back.reshape(COLS * OWN, FEATURES)
    return (rows[None, :, :WIDTH], rows[None, :, WIDTH:2 * WIDTH], share[:, :HD], share[:, HD:])


def solution(mesh):
    split = Mesh(mesh.devices.reshape(4, 4, 4, 4, 2), SPLIT)
    isl = ("zh", "core")
    placed = (
        P(isl, CTX, None),
        P(isl, CTX, None),
        P(isl, CTX, None),
        P(SPLIT, None),
        P(SPLIT, None),
        P(isl, None),
    )
    return jax.shard_map(
        per_device,
        mesh=split,
        in_specs=placed,
        out_specs=(
            P(isl, CTX, None),
            P(isl, CTX, None),
            P(SPLIT, None),
            P(SPLIT, None),
        ),
        check_vma=False,
    )
```

```python
import math

import jax
import jax.numpy as jnp
from jax import lax
from jax.experimental import pallas as pl
from jax.experimental.pallas import tpu as pltpu
from jax.sharding import Mesh, PartitionSpec as P

HD = 128
QPK = 8
WIDTH = QPK * HD
COLS = 64
OWN = 4
BLOCKS = 3

SPLIT = ("y", "zl", "x", "zh", "core")
CTX = ("y", "zl", "x")
PEERS = ("zl", "x", "y")
PLANE = ("x", "y")
LINE = ("zl", "zh")
last_dims = (((1,), (1,)), ((), ()))
plain_dims = (((1,), (0,)), ((), ()))
first_dims = (((0,), (0,)), ((), ()))
hidden = -1e30
FEATURES = 2 * WIDTH + 2 * BLOCKS * HD
vmem = pl.BlockSpec(memory_space=pltpu.VMEM)
smem = pl.BlockSpec(memory_space=pltpu.SMEM)
roomy = pltpu.CompilerParams(vmem_limit_bytes=40 * 1024 * 1024)


def attention_kernel(begin_ref, first_ref, sent_ref, back_ref, got_ref, bias_ref, dkey_ref, dvalue_ref):
    rows = COLS * OWN
    keys = BLOCKS * rows
    first = first_ref[0]
    got_ref[...] = sent_ref[...].reshape(rows, FEATURES)
    scale = float(HD) ** -0.5
    factor = scale * math.log2(math.e)

    def position(row):
        return ((row & 3) << 6) + (((row >> 2) & 3) << 4) + ((row >> 6) << 2) + ((row >> 4) & 3)

    row = lax.broadcasted_iota(jnp.int32, (1, rows), 1)
    start = jnp.zeros((1, rows), jnp.int32)
    for i in range(OWN):
        start = jnp.where((row & 3) == i, (begin_ref[i] - first) * COLS, start)
    key_pos = position(lax.broadcasted_iota(jnp.int32, (rows, 1), 0))
    for k in range(BLOCKS):
        shifted = key_pos - (BLOCKS - 1 - k) * OWN * COLS
        allowed = shifted >= start
        if k == BLOCKS - 1:
            allowed = allowed & (shifted <= position(row))
        bias_ref[k * rows:(k + 1) * rows] = jnp.where(allowed, 0.0, hidden).astype(jnp.float32)

    def window(place):
        parts = [got_ref[:, 2 * WIDTH + (2 * k + place) * HD:][:, :HD] for k in range(BLOCKS)]
        return jnp.concatenate(parts, axis=0)

    key, value = window(0), window(1)
    key_t, value_t = key.T, value.T
    held = {}

    def query(head):
        return got_ref[:, head * HD:(head + 1) * HD]

    def grad(head):
        return got_ref[:, WIDTH + head * HD:WIDTH + (head + 1) * HD]

    def put(at, block):
        back_ref[:, :, at:at + HD] = block.astype(jnp.bfloat16).reshape(COLS, OWN, HD)

    def add(ref, head, term):
        if head:
            ref[...] += term
        else:
            ref[...] = term

    def score(head):
        held["score", head] = lax.dot_general(key, query(head), last_dims, preferred_element_type=jnp.float32)

    def softmax(head):
        scaled = held.pop(("score", head)) * factor + bias_ref[...]
        expo = jnp.exp2(scaled - jnp.max(scaled, axis=0, keepdims=True))
        held["probs", head] = expo * (1.0 / jnp.sum(expo, axis=0, keepdims=True))
        held["low", head] = held["probs", head].astype(jnp.bfloat16)

    def dvalues(head):
        add(dvalue_ref, head, lax.dot_general(held.pop(("low", head)), grad(head), plain_dims, preferred_element_type=jnp.float32))

    def dprobs(head):
        held["dprobs", head] = lax.dot_general(value, grad(head), last_dims, preferred_element_type=jnp.float32)

    def output(head):
        out_t = lax.dot_general(value_t, held["low", head], plain_dims, preferred_element_type=jnp.float32).astype(jnp.bfloat16)
        put(head * HD, out_t.T)
        product = grad(head).T.astype(jnp.float32) * out_t.astype(jnp.float32)
        held["delta", head] = jnp.sum(product, axis=0, keepdims=True)

    def dscores(head):
        difference = held.pop(("dprobs", head)) - held.pop(("delta", head))
        held["dscores", head] = (held.pop(("probs", head)) * difference).astype(jnp.bfloat16)

    def dqueries(head):
        dscore = held.pop(("dscores", head))
        dquery_t = lax.dot_general(key_t, dscore, plain_dims, preferred_element_type=jnp.float32) * scale
        put(WIDTH + head * HD, dquery_t.astype(jnp.bfloat16).T)
        add(dkey_ref, head, lax.dot_general(dscore, query(head), plain_dims, preferred_element_type=jnp.float32))

    order = ((score, 0), (softmax, 1), (dvalues, 2), (dprobs, 1), (output, 1), (dqueries, 2), (dscores, 1))
    for turn in range(QPK + 2):
        for step, lag in order:
            if 0 <= turn - lag < QPK:
                step(turn - lag)
    for k in range(BLOCKS):
        block = slice(k * rows, (k + 1) * rows)
        put(2 * WIDTH + 2 * k * HD, dkey_ref[block] * scale)
        put(2 * WIDTH + (2 * k + 1) * HD, dvalue_ref[block])


def attention(begins, first, sent):
    rows = COLS * OWN
    keys = BLOCKS * rows
    return pl.pallas_call(
        attention_kernel,
        out_shape=jax.ShapeDtypeStruct(sent.shape, jnp.bfloat16),
        in_specs=[smem, smem, vmem],
        out_specs=vmem,
        scratch_shapes=[
            pltpu.VMEM((rows, FEATURES), jnp.bfloat16),
            pltpu.VMEM((keys, rows), jnp.float32),
            pltpu.VMEM((keys, HD), jnp.float32),
            pltpu.VMEM((keys, HD), jnp.float32),
        ],
        compiler_params=roomy,
        cost_estimate=pl.CostEstimate(
            flops=10 * rows * keys * HD * QPK, bytes_accessed=4 * sent.size, transcendentals=rows * keys * QPK
        ),
    )(begins, first, sent)


def split_kernel(core_ref, x_ref, keep_ref, send_ref):
    core = core_ref[0]
    tokens = x_ref.shape[0]
    for group in range(16):
        y, zl = divmod(group, 4)
        turned = x_ref[:, group * 256:(group + 1) * 256].astype(jnp.float32).T.reshape(16, 16, tokens)
        lower = turned[:, :8].reshape(128, tokens)
        upper = turned[:, 8:].reshape(128, tokens)
        keep = jnp.where(core == 0, lower, upper).astype(jnp.bfloat16)
        send = jnp.where(core == 0, upper, lower).astype(jnp.bfloat16)
        for x in range(4):
            at = (x * 4 + y) * 128 + zl * 32
            keep_ref[at:at + 32, :] = keep[x * 32:(x + 1) * 32]
            send_ref[at:at + 32, :] = send[x * 32:(x + 1) * 32]


def split_features(core, inputs):
    rows, width = inputs.shape
    shape = jax.ShapeDtypeStruct((width // 2, rows), jnp.bfloat16)
    return pl.pallas_call(
        split_kernel,
        out_shape=(shape, shape),
        in_specs=[smem, vmem],
        out_specs=(vmem, vmem),
        compiler_params=roomy,
        cost_estimate=pl.CostEstimate(flops=4 * inputs.size, bytes_accessed=4 * inputs.size, transcendentals=0),
    )(core, inputs)


def pack_kernel(q_ref, g_ref, mine_ref, other_ref, sent_ref):
    sent_ref[:, :, :WIDTH] = q_ref[...].reshape(COLS, OWN, WIDTH)
    sent_ref[:, :, WIDTH:2 * WIDTH] = g_ref[...].reshape(COLS, OWN, WIDTH)
    kv = (mine_ref[...] + other_ref[...]).astype(jnp.bfloat16).reshape(COLS, OWN, 2 * HD)
    for k in range(BLOCKS):
        back = BLOCKS - 1 - k
        at = 2 * WIDTH + 2 * k * HD
        if back:
            sent_ref[:back, :, at:at + 2 * HD] = jnp.zeros((back, OWN, 2 * HD), jnp.bfloat16)
        sent_ref[back:, :, at:at + 2 * HD] = kv[:COLS - back]


def pack(queries, grads, mine, other):
    return pl.pallas_call(
        pack_kernel,
        out_shape=jax.ShapeDtypeStruct((COLS, OWN, FEATURES), jnp.bfloat16),
        in_specs=[vmem] * 4,
        out_specs=vmem,
        compiler_params=roomy,
        cost_estimate=pl.CostEstimate(flops=mine.size, bytes_accessed=8 * queries.size, transcendentals=0),
    )(queries, grads, mine, other)


def fold_kernel(back_ref, dkv_ref):
    def part(k):
        at = 2 * WIDTH + 2 * k * HD
        return back_ref[:, :, at:at + 2 * HD].astype(jnp.float32)

    total = part(BLOCKS - 1)
    for k in range(1, BLOCKS):
        fill = jnp.zeros((k, OWN, 2 * HD), jnp.float32)
        total = total + jnp.concatenate([part(BLOCKS - 1 - k)[k:], fill], axis=0)
    dkv_ref[...] = total.reshape(COLS * OWN, 2 * HD).astype(jnp.bfloat16)


def fold(back):
    return pl.pallas_call(
        fold_kernel,
        out_shape=jax.ShapeDtypeStruct((COLS * OWN, 2 * HD), jnp.bfloat16),
        in_specs=[vmem],
        out_specs=vmem,
        compiler_params=roomy,
        cost_estimate=pl.CostEstimate(flops=back.size, bytes_accessed=back.size, transcendentals=0),
    )(back)


def exchange(array, axes):
    return lax.all_to_all(array, axes, split_axis=0, concat_axis=0, tiled=True)


def spread(array, axes):
    count = lax.axis_size(axes)
    return exchange(jnp.broadcast_to(array[None], (count,) + array.shape), axes)


def swap(array):
    return lax.ppermute(array, "core", [(0, 1), (1, 0)])


def per_device(layer_input, queries, grad_out, key_weight, value_weight, doc_len):
    inputs = layer_input[0]
    core = lax.axis_index("core").astype(jnp.int32).reshape(1)

    line = spread(jnp.concatenate([key_weight, value_weight], axis=1), LINE)
    keep, send = split_features(core, inputs)
    line, keep, send = lax.optimization_barrier((line, keep, send))
    weight = spread(line, PLANE).reshape(keep.shape[0], 2 * HD)

    weight, lengths = lax.optimization_barrier((weight, doc_len[0]))

    other = lax.dot_general(send, swap(weight), first_dims, preferred_element_type=jnp.float32)
    mine = lax.dot_general(keep, weight, first_dims, preferred_element_type=jnp.float32)

    first = lax.axis_index(PEERS).astype(jnp.int32) * OWN
    units = first + jnp.arange(OWN, dtype=jnp.int32)
    numbers = jnp.arange(lengths.shape[0], dtype=jnp.int32)
    ends = jnp.sum(jnp.where(numbers[None, :] <= numbers[:, None], lengths[None, :], 0), axis=1)
    begins = jnp.max(jnp.where(ends[None, :] <= units[:, None], ends[None, :], 0), axis=1)
    first = first.reshape(1)

    sent = exchange(pack(queries[0], grad_out[0], mine, other), PEERS)
    back = exchange(attention(begins, first, sent), PEERS)

    dkv = fold(back)
    away = jnp.dot(send, dkv, preferred_element_type=jnp.float32).astype(jnp.bfloat16)
    part = jnp.dot(keep, dkv, preferred_element_type=jnp.float32) + swap(away).astype(jnp.float32)
    part = part.astype(jnp.bfloat16).reshape(16, -1, 2 * HD)
    plane = jnp.sum(exchange(part, PLANE).astype(jnp.float32), axis=0).reshape(16, -1, 2 * HD)
    share = jnp.sum(exchange(plane, LINE), axis=0)

    rows = back.reshape(COLS * OWN, FEATURES)
    return (rows[None, :, :WIDTH], rows[None, :, WIDTH:2 * WIDTH], share[:, :HD], share[:, HD:])


def solution(mesh):
    split = Mesh(mesh.devices.reshape(4, 4, 4, 4, 2), SPLIT)
    isl = ("zh", "core")
    placed = (
        P(isl, CTX, None),
        P(isl, CTX, None),
        P(isl, CTX, None),
        P(SPLIT, None),
        P(SPLIT, None),
        P(isl, None),
    )
    return jax.shard_map(
        per_device,
        mesh=split,
        in_specs=placed,
        out_specs=(
            P(isl, CTX, None),
            P(isl, CTX, None),
            P(SPLIT, None),
            P(SPLIT, None),
        ),
        check_vma=False,
    )
```

```python
import math

import jax
import jax.numpy as jnp
from jax import lax
from jax.experimental import pallas as pl
from jax.experimental.pallas import tpu as pltpu
from jax.sharding import Mesh, PartitionSpec as P

HD = 128
QPK = 8
WIDTH = QPK * HD
COLS = 64
OWN = 4
BLOCKS = 3

SPLIT = ("y", "zl", "x", "zh", "core")
CTX = ("y", "zl", "x")
PEERS = ("zl", "x", "y")
PLANE = ("x", "y")
LINE = ("zl", "zh")
last_dims = (((1,), (1,)), ((), ()))
plain_dims = (((1,), (0,)), ((), ()))
first_dims = (((0,), (0,)), ((), ()))
hidden = -1e30
FEATURES = 2 * WIDTH + 2 * BLOCKS * HD
vmem = pl.BlockSpec(memory_space=pltpu.VMEM)
smem = pl.BlockSpec(memory_space=pltpu.SMEM)
roomy = pltpu.CompilerParams(vmem_limit_bytes=40 * 1024 * 1024)


def attention_kernel(begin_ref, first_ref, sent_ref, back_ref, got_ref, bias_ref, dkey_ref, dvalue_ref):
    rows = COLS * OWN
    keys = BLOCKS * rows
    first = first_ref[0]
    got_ref[...] = sent_ref[...].reshape(rows, FEATURES)
    scale = float(HD) ** -0.5
    factor = scale * math.log2(math.e)

    def position(row):
        return ((row & 3) << 6) + (((row >> 2) & 3) << 4) + ((row >> 6) << 2) + ((row >> 4) & 3)

    row = lax.broadcasted_iota(jnp.int32, (1, rows), 1)
    start = jnp.zeros((1, rows), jnp.int32)
    for i in range(OWN):
        start = jnp.where((row & 3) == i, (begin_ref[i] - first) * COLS, start)
    key_pos = position(lax.broadcasted_iota(jnp.int32, (rows, 1), 0))
    for k in range(BLOCKS):
        shifted = key_pos - (BLOCKS - 1 - k) * OWN * COLS
        allowed = shifted >= start
        if k == BLOCKS - 1:
            allowed = allowed & (shifted <= position(row))
        bias_ref[k * rows:(k + 1) * rows] = jnp.where(allowed, 0.0, hidden).astype(jnp.float32)

    def window(place):
        parts = [got_ref[:, 2 * WIDTH + (2 * k + place) * HD:][:, :HD] for k in range(BLOCKS)]
        return jnp.concatenate(parts, axis=0)

    key, value = window(0), window(1)
    key_t, value_t = key.T, value.T
    held = {}

    def query(head):
        return got_ref[:, head * HD:(head + 1) * HD]

    def grad(head):
        return got_ref[:, WIDTH + head * HD:WIDTH + (head + 1) * HD]

    def put(at, block):
        back_ref[:, :, at:at + HD] = block.astype(jnp.bfloat16).reshape(COLS, OWN, HD)

    def add(ref, head, term):
        if head:
            ref[...] += term
        else:
            ref[...] = term

    def score(head):
        held["score", head] = lax.dot_general(key, query(head), last_dims, preferred_element_type=jnp.float32)

    def softmax(head):
        scaled = held.pop(("score", head)) * factor + bias_ref[...]
        expo = jnp.exp2(scaled - jnp.max(scaled, axis=0, keepdims=True))
        held["probs", head] = expo * (1.0 / jnp.sum(expo, axis=0, keepdims=True))
        held["low", head] = held["probs", head].astype(jnp.bfloat16)

    def dvalues(head):
        add(dvalue_ref, head, lax.dot_general(held.pop(("low", head)), grad(head), plain_dims, preferred_element_type=jnp.float32))

    def dprobs(head):
        held["dprobs", head] = lax.dot_general(value, grad(head), last_dims, preferred_element_type=jnp.float32)

    def output(head):
        out_t = lax.dot_general(value_t, held["low", head], plain_dims, preferred_element_type=jnp.float32).astype(jnp.bfloat16)
        put(head * HD, out_t.T)
        product = grad(head).T.astype(jnp.float32) * out_t.astype(jnp.float32)
        held["delta", head] = jnp.sum(product, axis=0, keepdims=True)

    def dscores(head):
        difference = held.pop(("dprobs", head)) - held.pop(("delta", head))
        held["dscores", head] = (held.pop(("probs", head)) * difference).astype(jnp.bfloat16)

    def dqueries(head):
        dscore = held.pop(("dscores", head))
        dquery_t = lax.dot_general(key_t, dscore, plain_dims, preferred_element_type=jnp.float32) * scale
        put(WIDTH + head * HD, dquery_t.astype(jnp.bfloat16).T)
        add(dkey_ref, head, lax.dot_general(dscore, query(head), plain_dims, preferred_element_type=jnp.float32))

    order = ((score, 0), (softmax, 1), (dvalues, 2), (dprobs, 1), (output, 1), (dqueries, 2), (dscores, 1))
    for turn in range(QPK + 2):
        for step, lag in order:
            if 0 <= turn - lag < QPK:
                step(turn - lag)
    for k in range(BLOCKS):
        block = slice(k * rows, (k + 1) * rows)
        put(2 * WIDTH + 2 * k * HD, dkey_ref[block] * scale)
        put(2 * WIDTH + (2 * k + 1) * HD, dvalue_ref[block])


def attention(begins, first, sent):
    rows = COLS * OWN
    keys = BLOCKS * rows
    return pl.pallas_call(
        attention_kernel,
        out_shape=jax.ShapeDtypeStruct(sent.shape, jnp.bfloat16),
        in_specs=[smem, smem, vmem],
        out_specs=vmem,
        scratch_shapes=[
            pltpu.VMEM((rows, FEATURES), jnp.bfloat16),
            pltpu.VMEM((keys, rows), jnp.float32),
            pltpu.VMEM((keys, HD), jnp.float32),
            pltpu.VMEM((keys, HD), jnp.float32),
        ],
        compiler_params=roomy,
        cost_estimate=pl.CostEstimate(
            flops=10 * rows * keys * HD * QPK, bytes_accessed=4 * sent.size, transcendentals=rows * keys * QPK
        ),
    )(begins, first, sent)


def split_kernel(core_ref, x_ref, keep_ref, send_ref):
    core = core_ref[0]
    tokens = x_ref.shape[0]
    for group in range(16):
        y, zl = divmod(group, 4)
        turned = x_ref[:, group * 256:(group + 1) * 256].astype(jnp.float32).T.reshape(16, 16, tokens)
        lower = turned[:, :8].reshape(128, tokens)
        upper = turned[:, 8:].reshape(128, tokens)
        keep = jnp.where(core == 0, lower, upper).astype(jnp.bfloat16)
        send = jnp.where(core == 0, upper, lower).astype(jnp.bfloat16)
        for x in range(4):
            at = (x * 4 + y) * 128 + zl * 32
            keep_ref[at:at + 32, :] = keep[x * 32:(x + 1) * 32]
            send_ref[at:at + 32, :] = send[x * 32:(x + 1) * 32]


def split_features(core, inputs):
    rows, width = inputs.shape
    shape = jax.ShapeDtypeStruct((width // 2, rows), jnp.bfloat16)
    return pl.pallas_call(
        split_kernel,
        out_shape=(shape, shape),
        in_specs=[smem, vmem],
        out_specs=(vmem, vmem),
        compiler_params=roomy,
        cost_estimate=pl.CostEstimate(flops=4 * inputs.size, bytes_accessed=4 * inputs.size, transcendentals=0),
    )(core, inputs)


def pack_kernel(q_ref, g_ref, mine_ref, other_ref, sent_ref):
    sent_ref[:, :, :WIDTH] = q_ref[...].reshape(COLS, OWN, WIDTH)
    sent_ref[:, :, WIDTH:2 * WIDTH] = g_ref[...].reshape(COLS, OWN, WIDTH)
    kv = (mine_ref[...] + other_ref[...]).astype(jnp.bfloat16).reshape(COLS, OWN, 2 * HD)
    for k in range(BLOCKS):
        back = BLOCKS - 1 - k
        at = 2 * WIDTH + 2 * k * HD
        if back:
            sent_ref[:back, :, at:at + 2 * HD] = jnp.zeros((back, OWN, 2 * HD), jnp.bfloat16)
        sent_ref[back:, :, at:at + 2 * HD] = kv[:COLS - back]


def pack(queries, grads, mine, other):
    return pl.pallas_call(
        pack_kernel,
        out_shape=jax.ShapeDtypeStruct((COLS, OWN, FEATURES), jnp.bfloat16),
        in_specs=[vmem] * 4,
        out_specs=vmem,
        compiler_params=roomy,
        cost_estimate=pl.CostEstimate(flops=mine.size, bytes_accessed=8 * queries.size, transcendentals=0),
    )(queries, grads, mine, other)


def fold_kernel(back_ref, dkv_ref):
    def part(k):
        at = 2 * WIDTH + 2 * k * HD
        return back_ref[:, :, at:at + 2 * HD].astype(jnp.float32)

    total = part(BLOCKS - 1)
    for k in range(1, BLOCKS):
        fill = jnp.zeros((k, OWN, 2 * HD), jnp.float32)
        total = total + jnp.concatenate([part(BLOCKS - 1 - k)[k:], fill], axis=0)
    dkv_ref[...] = total.reshape(COLS * OWN, 2 * HD).astype(jnp.bfloat16)


def fold(back):
    return pl.pallas_call(
        fold_kernel,
        out_shape=jax.ShapeDtypeStruct((COLS * OWN, 2 * HD), jnp.bfloat16),
        in_specs=[vmem],
        out_specs=vmem,
        compiler_params=roomy,
        cost_estimate=pl.CostEstimate(flops=back.size, bytes_accessed=back.size, transcendentals=0),
    )(back)


def exchange(array, axes):
    return lax.all_to_all(array, axes, split_axis=0, concat_axis=0, tiled=True)


def spread(array, axes):
    count = lax.axis_size(axes)
    return exchange(jnp.broadcast_to(array[None], (count,) + array.shape), axes)


def swap(array):
    return lax.ppermute(array, "core", [(0, 1), (1, 0)])


def per_device(layer_input, queries, grad_out, key_weight, value_weight, doc_len):
    inputs = layer_input[0]
    core = lax.axis_index("core").astype(jnp.int32).reshape(1)
    place = lax.axis_index(PEERS)
    ends = jnp.cumsum(doc_len[0])
    units = place * OWN + jnp.arange(OWN, dtype=jnp.int32)
    begins = jnp.max(jnp.where(ends[None, :] <= units[:, None], ends[None, :], 0), axis=1)
    first = (place * OWN).astype(jnp.int32).reshape(1)

    line = spread(jnp.concatenate([key_weight, value_weight], axis=1), LINE)
    keep, send = split_features(core, inputs)
    line, keep, send, begins, first = lax.optimization_barrier((line, keep, send, begins, first))
    weight = spread(line, PLANE).reshape(keep.shape[0], 2 * HD)

    other = lax.dot_general(send, swap(weight), first_dims, preferred_element_type=jnp.float32)
    mine = lax.dot_general(keep, weight, first_dims, preferred_element_type=jnp.float32)

    sent = exchange(pack(queries[0], grad_out[0], mine, other), PEERS)
    back = exchange(attention(begins, first, sent), PEERS)

    dkv = fold(back)
    away = jnp.dot(send, dkv, preferred_element_type=jnp.float32).astype(jnp.bfloat16)
    part = jnp.dot(keep, dkv, preferred_element_type=jnp.float32) + swap(away).astype(jnp.float32)
    part = part.astype(jnp.bfloat16).reshape(16, -1, 2 * HD)
    plane = jnp.sum(exchange(part, PLANE).astype(jnp.float32), axis=0).reshape(16, -1, 2 * HD)
    share = jnp.sum(exchange(plane, LINE), axis=0)

    rows = back.reshape(COLS * OWN, FEATURES)
    return (rows[None, :, :WIDTH], rows[None, :, WIDTH:2 * WIDTH], share[:, :HD], share[:, HD:])


def solution(mesh):
    split = Mesh(mesh.devices.reshape(4, 4, 4, 4, 2), SPLIT)
    isl = ("zh", "core")
    placed = (
        P(isl, CTX, None),
        P(isl, CTX, None),
        P(isl, CTX, None),
        P(SPLIT, None),
        P(SPLIT, None),
        P(isl, None),
    )
    return jax.shard_map(
        per_device,
        mesh=split,
        in_specs=placed,
        out_specs=(
            P(isl, CTX, None),
            P(isl, CTX, None),
            P(SPLIT, None),
            P(SPLIT, None),
        ),
        check_vma=False,
    )
```
